512 devices in a mesh: blk: 64 (over z_hi, y, core), rel: 8 (over z_lo, x).
Axes of the slice: x: 4, y: 8, z: 8 (z_hi: 4, z_lo: 2; z = z_hi * 2 + z_lo), core: 2. Of those that a mesh axis runs over, the one named last changes fastest.
Arguments:
- source_table: float32 [400, 393216], P(None, ('blk', 'rel')), may hold values from -1.2 to 1.2
- source_state: float32 [393216], P(('blk', 'rel')), may hold values from 0.001 to 0.1
- target_table: float32 [400, 393216], P(None, ('blk', 'rel')), may hold values from -1.2 to 1.2
- target_state: float32 [393216], P(('blk', 'rel')), may hold values from 0.001 to 0.1
- relation_ops: float32 [400, 8192], P(None, 'blk'), may hold values from 0.5 to 1.5
- relation_state: float32 [400, 8192], P(None, 'blk'), may hold values from 0.01 to 1
- source_ids: int32 [2, 262144], P(None, ('blk', 'rel')), may hold values from 0 to 767
- target_ids: int32 [2, 262144], P(None, ('blk', 'rel')), may hold values from 0 to 767
- relation_ids: int32 [2, 262144], P(None, ('blk', 'rel')), may hold values from 0 to 127
- negative_ids: int32 [2, 262144], P(None, ('blk', 'rel')), may hold values from 0 to 767
Outputs:
- new_source: float32 [400, 393216], P(None, ('blk', 'rel'))
- new_source_state: float32 [393216], P(('blk', 'rel'))
- held_target: float32 [400, 393216], P(None, ('blk', 'rel'))
- held_target_state: float32 [393216], P(('blk', 'rel'))
- new_relations: float32 [400, 8192], P(None, 'blk')
- new_relation_state: float32 [400, 8192], P(None, 'blk')
The draws below stay inside these ranges and needn't reach their ends.
All inputs are finite; a program needn't handle non-finite values.
Results may differ from the reference program's by a relative error of at most 0.0001.
Values sent between devices are 32-bit elements; how exact they have to be, the bound alone decides.
No kernel may reach another device: no remote copies, remote signals or barrier semaphores. Data moves between devices by JAX's collectives and lax.ppermute only.
A program may use at most 64 MiB of HBM per device.

```python
import math
import jax
import jax.numpy as jnp
from jax import lax

D = 400
ROWS = 768
EDGE_DEV = 512
NEG_DEV = 512
REL_DEV = 128
BUCKETS = 2
ENTITIES = 393216
EDGES = 262144
NEGS = 262144
RELS = 8192
N_BLK = 64
N_REL = 8


def touch_ends(entries, own_key, low, top_value):
    spot = [jax.random.randint(jax.random.fold_in(own_key, axis), (), 0, length) for axis, length in enumerate(entries.shape)]
    main_axis = entries.shape.index(max(entries.shape))
    beside = spot[:main_axis] + [(spot[main_axis] + 1) % entries.shape[main_axis]] + spot[main_axis + 1:]
    return entries.at[tuple(spot)].set(low).at[tuple(beside)].set(top_value)


def shard_levels(rng, shape, split, smallest, high):
    def one(dim, blocks):
        heights = jax.random.uniform(jax.random.fold_in(jax.random.fold_in(rng, 6), dim), (blocks,), jnp.float32, smallest / len(split), high / len(split))
        return jnp.repeat(jnp.exp(heights), shape[dim] // blocks).reshape((-1,) + (1,) * (len(shape) - dim - 1))

    gain = one(*split[0])
    for cut in split[1:]:
        gain = gain * one(*cut)
    return gain


def bell_draw(rng, shape, deviation, limit, shards=(), dtype=jnp.bfloat16):
    gain = shard_levels(rng, shape, shards, -0.22, 0.18) if shards else 1.0
    drawn = jax.random.normal(rng, shape, jnp.float32) * deviation * gain
    return jnp.minimum(jnp.maximum(drawn, -limit), limit).astype(dtype)


def setup_inputs(seed: int = 0) -> dict:
    streams_of = jax.random.split(jax.random.key(seed), 11)
    source_table = bell_draw(streams_of[0], (D, ENTITIES), 0.2, 1.2, ((1, 512),), jnp.float32)
    source_state = jnp.clip(jnp.exp(math.log(0.1) - 4.6051702 * jax.random.uniform(streams_of[1], (ENTITIES,), jnp.float32) ** shard_levels(streams_of[1], (ENTITIES,), ((0, 512),), -0.2, 0.2)), 0.001, 0.1)
    target_table = bell_draw(streams_of[2], (D, ENTITIES), 0.2, 1.2, ((1, 512),), jnp.float32)
    target_state = jnp.clip(jnp.exp(math.log(0.1) - 4.6051702 * jax.random.uniform(streams_of[3], (ENTITIES,), jnp.float32) ** shard_levels(streams_of[3], (ENTITIES,), ((0, 512),), -0.2, 0.2)), 0.001, 0.1)
    relation_ops = jnp.clip(0.5 + 1.0 * jax.random.uniform(streams_of[4], (D, RELS), jnp.float32) ** shard_levels(streams_of[4], (D, RELS), ((1, 64),), -0.2, 0.2), 0.5, 1.5)
    relation_state = jnp.clip(jnp.exp(math.log(1.0) - 4.6051702 * jax.random.uniform(streams_of[5], (D, RELS), jnp.float32) ** shard_levels(streams_of[5], (D, RELS), ((1, 64),), -0.2, 0.2)), 0.01, 1.0)
    source_ids = touch_ends(jax.random.randint(streams_of[6], (BUCKETS, EDGES), 0, ROWS), jax.random.fold_in(streams_of[6], 1), 0, ROWS - 1).astype(jnp.int32)
    target_ids = touch_ends(jax.random.randint(streams_of[7], (BUCKETS, EDGES), 0, ROWS), jax.random.fold_in(streams_of[7], 1), 0, ROWS - 1).astype(jnp.int32)
    relation_ids = touch_ends(jax.random.randint(streams_of[8], (BUCKETS, EDGES), 0, REL_DEV), jax.random.fold_in(streams_of[8], 1), 0, REL_DEV - 1).astype(jnp.int32)
    negative_ids = touch_ends(jax.random.randint(streams_of[9], (BUCKETS, NEGS), 0, ROWS), jax.random.fold_in(streams_of[9], 1), 0, ROWS - 1).astype(jnp.int32)
    return {"source_table": source_table, "source_state": source_state, "target_table": target_table, "target_state": target_state, "relation_ops": relation_ops, "relation_state": relation_state, "source_ids": source_ids, "target_ids": target_ids, "relation_ids": relation_ids, "negative_ids": negative_ids}


learn_rate = 0.1
epsilon = 1e-06
HIGHEST = lax.Precision.HIGHEST

def row_adagrad(matrix, row_state, gradient):
    fresh = row_state + lax.optimization_barrier(jnp.mean(gradient * gradient, axis=0))
    return (matrix - learn_rate * gradient / (jnp.sqrt(fresh) + epsilon)[None, :], fresh)

def slice_step(source_side, source_rows, target_side, target_rows, relations, source_idx, target_idx, relation_idx, negative_idx):
    source = jnp.take(source_side, source_idx, axis=1)
    target = jnp.take(target_side, target_idx, axis=1)
    negative = jnp.take(target_side, negative_idx, axis=1)
    relation = jnp.take(relations, relation_idx, axis=1)
    queries = source * relation
    positive = lax.optimization_barrier(jnp.sum(queries * target, axis=0))
    neg_score = lax.dot_general(queries, negative, (((0,), (0,)), ((), ())), precision=HIGHEST)
    pos_coef = -jax.nn.sigmoid(-positive)
    neg_coef = jax.nn.sigmoid(neg_score) / negative_idx.shape[0]
    grad_query = target * pos_coef[None, :] + lax.dot_general(negative, neg_coef, (((1,), (1,)), ((), ())), precision=HIGHEST)
    grad_target = queries * pos_coef[None, :]
    grad_negative = jnp.dot(queries, neg_coef, precision=HIGHEST)
    target_grad = jnp.zeros_like(target_side).at[:, target_idx].add(grad_target).at[:, negative_idx].add(grad_negative)
    source_grad = jnp.zeros_like(source_side).at[:, source_idx].add(grad_query * relation)
    relation_grad = jnp.zeros_like(relations).at[:, relation_idx].add(grad_query * source)
    new_target, new_target_rows = row_adagrad(target_side, target_rows, target_grad)
    new_source, new_source_rows = row_adagrad(source_side, source_rows, source_grad)
    return (new_source, new_source_rows, new_target, new_target_rows, relation_grad)

def reference(source_table, source_state, target_table, target_state, relation_ops, relation_state, source_ids, target_ids, relation_ids, negative_ids):
    slice_count = N_BLK * N_REL

    def split_table(matrix):
        return matrix.reshape(D, slice_count, ROWS).transpose(1, 0, 2)

    def join_table(blocks):
        return blocks.transpose(1, 0, 2).reshape(D, slice_count * ROWS)
    source_blocks = split_table(source_table)
    source_rows = source_state.reshape(slice_count, ROWS)
    target_blocks = split_table(target_table)
    target_rows = target_state.reshape(slice_count, ROWS)
    relation_blocks = relation_ops.reshape(D, N_BLK, REL_DEV).transpose(1, 0, 2)
    source_split = source_ids.reshape(BUCKETS, slice_count, EDGE_DEV)
    target_split = target_ids.reshape(BUCKETS, slice_count, EDGE_DEV)
    relation_split = relation_ids.reshape(BUCKETS, slice_count, EDGE_DEV)
    negative_split = negative_ids.reshape(BUCKETS, slice_count, NEG_DEV)
    owners = (jnp.arange(slice_count) // N_REL).astype(jnp.int32)
    summed = jnp.zeros((N_BLK, D, REL_DEV), jnp.float32)

    def per_slice(items):
        src_side, src_rows, tgt_side, tgt_rows, owner, src_idx, tgt_idx, rel_idx, neg_idx = items
        return slice_step(src_side, src_rows, tgt_side, tgt_rows, relation_blocks[owner], src_idx, tgt_idx, rel_idx, neg_idx)
    for bucket in range(BUCKETS):
        if bucket > 0:
            target_blocks = jnp.roll(target_blocks, N_REL, axis=0)
            target_rows = jnp.roll(target_rows, N_REL, axis=0)
        source_blocks, source_rows, target_blocks, target_rows, relation_grads = lax.map(per_slice, (source_blocks, source_rows, target_blocks, target_rows, owners, source_split[bucket], target_split[bucket], relation_split[bucket], negative_split[bucket]))
        summed = summed + relation_grads.reshape(N_BLK, N_REL, D, REL_DEV).sum(axis=1)
    summed_flat = summed.transpose(1, 0, 2).reshape(D, N_BLK * REL_DEV)
    new_relation_state = relation_state + summed_flat * summed_flat
    new_relations = relation_ops - learn_rate * summed_flat / (jnp.sqrt(new_relation_state) + epsilon)
    return (join_table(source_blocks), source_rows.reshape(slice_count * ROWS), join_table(target_blocks), target_rows.reshape(slice_count * ROWS), new_relations, new_relation_state)
```

```python
import functools

import jax
import jax.numpy as jnp
from jax import lax
from jax.experimental import pallas as pl
from jax.experimental.pallas import tpu as pltpu
from jax.sharding import PartitionSpec as P

LR = 0.1
EPS = 1e-06
F32 = jnp.float32
BF16 = jnp.bfloat16
VMEM_LIMIT = 32 * 1024 * 1024
TILE = 256
NEAR = 512


def split(x):
    hi = x.astype(BF16)
    lo = (x - hi.astype(F32)).astype(BF16)
    return hi, lo


def dot(a, b):
    return jnp.dot(a, b, preferred_element_type=F32)


def dot_nt(a, b):
    return lax.dot_general(a, b, (((1,), (1,)), ((), ())), preferred_element_type=F32)


def column(row):
    n = row.shape[1]
    return jnp.transpose(jnp.broadcast_to(row, (8, n)))[:, 0:1]


def hot_down(row, length):
    n = row.shape[1]
    spots = lax.broadcasted_iota(jnp.int32, (length, n), 0)
    return jnp.where(spots == row, 1.0, 0.0).astype(BF16)


def hot_along(col, length, start=0):
    n = col.shape[0]
    spots = lax.broadcasted_iota(jnp.int32, (n, length), 1) + start
    return jnp.where(spots == col, 1.0, 0.0).astype(BF16)


def picked(matrix, hot):
    hi, lo = split(matrix)
    return dot(hi, hot) + dot(lo, hot)


def weights(q_t, t, target_col, negative_col, start, negatives):
    (qa, qb), (ta, tb) = q_t, split(t)
    score = dot(qa, ta) + dot(qa, tb) + dot(qb, ta)
    spots = lax.broadcasted_iota(jnp.int32, score.shape, 1) + start
    count = jnp.sum(jnp.where(spots == negative_col, 1.0 / negatives, 0.0), axis=0, keepdims=True)
    level = jax.nn.sigmoid(score)
    return level * count + jnp.where(spots == target_col, level - 1.0, 0.0)


def stepped(matrix, state, grad):
    fresh = state + jnp.sum(grad * grad, axis=0, keepdims=True) * (1.0 / grad.shape[0])
    return matrix - grad * (LR / (jnp.sqrt(fresh) + EPS)), fresh


def started(copies):
    out = [pltpu.make_async_copy(src, dst, sem) for src, dst, sem in copies]
    for c in out:
        c.start()
    return out


def near_body(bucket, s_in, t_in, tst_in, r_in, sid_in, tid_in, rid_in, nid_in,
              near_ref, src_ref, rel_ref, qa_ref, qb_ref, qta_ref, qtb_ref, wa_ref, wb_ref,
              s_ref, t_ref, tst_ref, r_ref, sid_ref, tid_ref, rid_ref, nid_ref, sems):
    d, rows = t_ref.shape
    c_sid, c_rid, c_r, c_s, c_tid, c_nid, c_tst, c_t = started([
        (sid_in, sid_ref, sems.at[0]), (rid_in, rid_ref, sems.at[1]), (r_in, r_ref, sems.at[2]),
        (s_in, s_ref, sems.at[3]), (tid_in, tid_ref, sems.at[4]), (nid_in, nid_ref, sems.at[5]),
        (tst_in, tst_ref, sems.at[6]), (t_in.at[:, 0:NEAR], t_ref.at[:, 0:NEAR], sems.at[7])])
    c_sid.wait()
    c_rid.wait()
    hot_s = hot_down(sid_ref[bucket:bucket + 1, :], rows)
    hot_r = hot_down(rid_ref[bucket:bucket + 1, :], r_ref.shape[1])
    c_r.wait()
    rel = picked(r_ref[...], hot_r)
    c_s.wait()
    src = picked(s_ref[...], hot_s)
    src_ref[...] = src
    rel_ref[...] = rel
    q = src * rel
    qa, qb = split(q)
    qa_ref[...] = qa
    qb_ref[...] = qb
    q_t = split(jnp.transpose(q))
    qta_ref[...], qtb_ref[...] = q_t
    c_tid.wait()
    c_nid.wait()
    target_col = column(tid_ref[bucket:bucket + 1, :])
    negative_col = column(nid_ref[bucket:bucket + 1, :])
    c_tst.wait()
    c_t.wait()
    for start in range(0, NEAR, TILE):
        cols = slice(start, start + TILE)
        t = t_ref[:, cols]
        wa, wb = split(weights(q_t, t, target_col, negative_col, start, nid_ref.shape[1]))
        wa_ref[:, cols] = wa
        wb_ref[:, cols] = wb
        grad = dot(qa, wa) + dot(qb, wa) + dot(qa, wb)
        t_new, fresh = stepped(t, tst_ref[cols][None], grad)
        near_ref[0:d, cols] = t_new
        near_ref[d:d + 8, cols] = jnp.broadcast_to(fresh, (8, TILE))


def far_body(bucket, t_in, tst_in, tid_in, nid_in, qa_ref, qb_ref, qta_ref, qtb_ref,
             far_ref, wa_ref, wb_ref,
             t_ref, tst_ref, tid_ref, nid_ref, sems):
    d = t_ref.shape[0]
    copies = started([
        (tid_in, tid_ref, sems.at[0]), (nid_in, nid_ref, sems.at[1]), (tst_in, tst_ref, sems.at[2]),
        (t_in.at[:, NEAR:], t_ref, sems.at[3])])
    for c in copies:
        c.wait()
    q_t = (qta_ref[...], qtb_ref[...])
    qa, qb = qa_ref[...], qb_ref[...]
    target_col = column(tid_ref[bucket:bucket + 1, :])
    negative_col = column(nid_ref[bucket:bucket + 1, :])
    t = t_ref[...]
    wa, wb = split(weights(q_t, t, target_col, negative_col, NEAR, nid_ref.shape[1]))
    wa_ref[...] = wa
    wb_ref[...] = wb
    grad = dot(qa, wa) + dot(qb, wa) + dot(qa, wb)
    t_new, fresh = stepped(t, tst_ref[NEAR:][None], grad)
    far_ref[0:d, :] = t_new
    far_ref[d:d + 8, :] = jnp.broadcast_to(fresh, (8, t.shape[1]))


def source_body(bucket, s_in, sst_in, t_in, r_in, sid_in, rid_in,
                src_ref, rel_ref, wna_ref, wnb_ref, wfa_ref, wfb_ref,
                snew_out, sst_out, rel2_out, qa_out, qb_out, rgrad_ref, src2_ref, qta_ref, qtb_ref,
                s_ref, sst_ref, t_ref, r_ref, sid_ref, rid_ref,
                snew_ref, sstnew_ref, rel2_ref, qa_ref, qb_ref, sems):
    d, rows = s_ref.shape
    copies = started([
        (t_in, t_ref, sems.at[0]), (sid_in, sid_ref, sems.at[1]), (rid_in, rid_ref, sems.at[2]),
        (r_in, r_ref, sems.at[3]), (s_in, s_ref, sems.at[4]), (sst_in, sst_ref, sems.at[5])])
    copies[0].wait()
    ta, tb = split(t_ref[:, 0:NEAR])
    gq = dot_nt(ta, wna_ref[...]) + dot_nt(tb, wna_ref[...]) + dot_nt(ta, wnb_ref[...])
    ta, tb = split(t_ref[:, NEAR:])
    gq += dot_nt(ta, wfa_ref[...]) + dot_nt(tb, wfa_ref[...]) + dot_nt(ta, wfb_ref[...])
    for c in copies[1:]:
        c.wait()
    rid_col = column(rid_ref[bucket:bucket + 1, :])
    sid_col = column(sid_ref[bucket:bucket + 1, :])
    rgrad_ref[...] = picked(gq * src_ref[...], hot_along(rid_col, r_ref.shape[1]))
    grad = picked(gq * rel_ref[...], hot_along(sid_col, rows))
    s_new, fresh = stepped(s_ref[...], sst_ref[...][None], grad)
    snew_ref[...] = s_new
    sstnew_ref[...] = fresh[0]
    outs = started([(snew_ref, snew_out, sems.at[6]), (sstnew_ref, sst_out, sems.at[7])])
    after = bucket + 1
    src = picked(s_new, hot_down(sid_ref[after:after + 1, :], rows))
    rel = picked(r_ref[...], hot_down(rid_ref[after:after + 1, :], r_ref.shape[1]))
    src2_ref[...] = src
    rel2_ref[...] = rel
    q = src * rel
    qa_ref[...], qb_ref[...] = split(q)
    outs += started([(rel2_ref, rel2_out, sems.at[8]), (qa_ref, qa_out, sems.at[9]), (qb_ref, qb_out, sems.at[10])])
    qta_ref[...], qtb_ref[...] = split(jnp.transpose(q))
    for c in outs:
        c.wait()


def query_body(bucket, direct_ref, relayed_ref, near_ref, src_ref, qta_ref, qtb_ref, rgrad_ref,
               tid_ref, rid_ref, nid_ref,
               gq_out, wa_out, wb_out, t_out, sum_ref,
               gq_ref, wa_ref, wb_ref, t_ref, sems):
    d = src_ref.shape[0]
    rows = t_ref.shape[1]
    q_t = (qta_ref[...], qtb_ref[...])
    target_col = column(tid_ref[bucket:bucket + 1, :])
    negative_col = column(nid_ref[bucket:bucket + 1, :])
    gq = jnp.zeros(src_ref.shape, F32)
    outs = []
    for start in range(0, rows, TILE):
        cols = slice(start, start + TILE)
        if start < NEAR:
            t_all = near_ref[:, cols]
        else:
            away = slice(start - NEAR, start - NEAR + TILE)
            t_all = direct_ref[:, away] + relayed_ref[:, away]
        t_ref[:, cols] = t_all
        t = t_all[0:d]
        wa, wb = split(weights(q_t, t, target_col, negative_col, start, nid_ref.shape[1]))
        wa_ref[:, cols] = wa
        wb_ref[:, cols] = wb
        ta, tb = split(t)
        gq += dot_nt(ta, wa) + dot_nt(tb, wa) + dot_nt(ta, wb)
    gq_ref[...] = gq
    outs = started([(gq_ref, gq_out, sems.at[0]), (wa_ref, wa_out, sems.at[1]), (wb_ref, wb_out, sems.at[2]),
                    (t_ref, t_out, sems.at[3])])
    rid_col = column(rid_ref[bucket:bucket + 1, :])
    total = rgrad_ref[...] + picked(gq * src_ref[...], hot_along(rid_col, rgrad_ref.shape[1]))
    sum_ref[0:d, :] = total
    if sum_ref.shape[0] > d:
        sum_ref[d:, :] = jnp.zeros((sum_ref.shape[0] - d, total.shape[1]), F32)
    for c in outs:
        c.wait()


def target_body(t_in, qa_in, qb_in, wa_in, wb_in, tnew_out, tst_out,
                t_ref, qa_ref, qb_ref, wa_ref, wb_ref, tnew_ref, tst_ref, sems):
    d, rows = tnew_ref.shape
    copies = started([
        (qa_in, qa_ref, sems.at[0]), (qb_in, qb_ref, sems.at[1]), (wa_in, wa_ref, sems.at[2]),
        (wb_in, wb_ref, sems.at[3]), (t_in, t_ref, sems.at[4])])
    for c in copies:
        c.wait()
    qa, qb = qa_ref[...], qb_ref[...]
    outs = []
    for i, start in enumerate(range(0, rows, TILE)):
        cols = slice(start, start + TILE)
        wa, wb = wa_ref[:, cols], wb_ref[:, cols]
        grad = dot(qa, wa) + dot(qb, wa) + dot(qa, wb)
        t_new, fresh = stepped(t_ref[0:d, cols], t_ref[d:d + 1, cols], grad)
        tnew_ref[:, cols] = t_new
        tst_ref[cols] = fresh[0]
        outs += started([(tnew_ref.at[:, cols], tnew_out.at[:, cols], sems.at[5 + i])])
    outs += started([(tst_ref, tst_out, sems.at[4])])
    for c in outs:
        c.wait()


def last_source_body(bucket, s_in, sst_in, gq_in, rel_in, sid_in, snew_out, sst_out,
                     s_ref, sst_ref, gq_ref, rel_ref, sid_ref, snew_ref, sstnew_ref, sems):
    d, rows = s_ref.shape
    copies = started([
        (gq_in, gq_ref, sems.at[0]), (rel_in, rel_ref, sems.at[1]), (sid_in, sid_ref, sems.at[2]),
        (s_in, s_ref, sems.at[3]), (sst_in, sst_ref, sems.at[4])])
    for c in copies:
        c.wait()
    sid_col = column(sid_ref[bucket:bucket + 1, :])
    ga, gb = split(gq_ref[...] * rel_ref[...])
    outs = []
    for i, start in enumerate(range(0, rows, TILE)):
        cols = slice(start, start + TILE)
        hot = hot_along(sid_col, TILE, start)
        s_new, fresh = stepped(s_ref[:, cols], sst_ref[cols][None], dot(ga, hot) + dot(gb, hot))
        snew_ref[:, cols] = s_new
        sstnew_ref[cols] = fresh[0]
        outs += started([(snew_ref.at[:, cols], snew_out.at[:, cols], sems.at[5 + i])])
    outs += started([(sstnew_ref, sst_out, sems.at[4])])
    for c in outs:
        c.wait()


def total_body(parts_ref, out_ref):
    own = parts_ref[0]
    for i in range(1, parts_ref.shape[0]):
        own += parts_ref[i]
    for i in range(out_ref.shape[0]):
        out_ref[i] = own


HBM, VM = pltpu.HBM, pltpu.VMEM


def call(body, ins, outs, scratch=(), flops=0):
    moved = sum(a.size * a.dtype.itemsize for _, a in (*ins, *outs))
    return pl.pallas_call(
        body,
        out_shape=[m(a.shape, a.dtype) for m, a in outs],
        in_specs=[pl.BlockSpec(memory_space=m) for m, _ in ins],
        out_specs=[pl.BlockSpec(memory_space=m) for m, _ in outs],
        scratch_shapes=list(scratch),
        compiler_params=pltpu.CompilerParams(vmem_limit_bytes=VMEM_LIMIT),
        cost_estimate=pl.CostEstimate(flops=flops, bytes_accessed=moved, transcendentals=0),
    )(*[pltpu.with_memory_space_constraint(a, m) for m, a in ins])


def of(spec, *arrays):
    return [(spec, a) for a in arrays]


def room(*arrays):
    return [pltpu.VMEM(a.shape, a.dtype) for a in arrays]


def per_device(s, sst, t, tst, r, rst, sid, tid, rid, nid):
    d, rows = s.shape
    edges = sid.shape[1]
    rels = r.shape[1]
    away = rows - NEAR
    shape = jax.ShapeDtypeStruct
    sems = pltpu.SemaphoreType.DMA((12,))
    wide = shape((d, edges), F32)
    thin = shape((d, edges), BF16)
    thin_t = shape((edges, d), BF16)
    full = shape((d, rows), F32)
    held = shape((d + 8, rows), F32)
    line = shape((rows,), F32)
    half = shape((edges, rows), BF16)
    near_w = shape((edges, NEAR), BF16)
    far_w = shape((edges, away), BF16)
    unit = 2 * d * rows * edges

    near, src0, rel0, qa0, qb0, qta0, qtb0, wna, wnb = call(
        functools.partial(near_body, 0),
        of(HBM, s, t, tst, r, sid, tid, rid, nid),
        of(VM, shape((d + 8, NEAR), F32), wide, wide, thin, thin, thin_t, thin_t, near_w, near_w),
        [*room(s, t, tst, r, sid, tid, rid, nid), sems], flops=7 * unit)
    far, wfa, wfb = call(
        functools.partial(far_body, 0),
        of(HBM, t, tst, tid, nid) + of(VM, qa0, qb0, qta0, qtb0),
        of(VM, shape((d + 8, away), F32), far_w, far_w),
        [pltpu.VMEM((d, away), F32), *room(tst, tid, nid), sems], flops=2 * unit)

    count = lax.axis_size("blk")
    run = 16
    ring = [(i, (i + 1) % count) for i in range(count)]
    turns = [p for p in ring if p[1] % run == 0]
    first_leg = [(a, (b + run - 2) % count) for a, b in turns]
    second_leg = [((b + run - 2) % count, b) for a, b in turns]
    near = lax.ppermute(near, "blk", ring)
    leg = lax.ppermute(far, "blk", first_leg)
    direct = lax.ppermute(far, "blk", [p for p in ring if p not in turns])
    s1, sst1, rel1, qa1, qb1, rgrad0, src1, qta1, qtb1 = call(
        functools.partial(source_body, 0),
        of(HBM, s, sst, t, r, sid, rid) + of(VM, src0, rel0, wna, wnb, wfa, wfb),
        of(HBM, full, line, wide, thin, thin) + of(VM, shape((d, rels), F32), wide, thin_t, thin_t),
        [*room(s, sst, t, r, sid, rid, full, line, wide, thin, thin), sems], flops=9 * unit)
    relayed = lax.ppermute(leg, "blk", second_leg)

    group = lax.axis_size("rel")
    piece = -(-d // (8 * group)) * 8
    gq1, wa1, wb1, t1, total = call(
        functools.partial(query_body, 1),
        of(VM, direct, relayed, near, src1, qta1, qtb1, rgrad0, tid, rid, nid),
        of(HBM, wide, half, half, held) + of(VM, shape((piece * group, rels), F32)),
        [*room(wide, half, half, held), sems], flops=7 * unit)
    parts = lax.all_to_all(total.reshape(group, piece, rels), "rel", 0, 0, tiled=True)
    t2, tst2 = call(
        target_body,
        of(HBM, t1, qa1, qb1, wa1, wb1),
        of(HBM, full, line),
        [*room(held, thin, thin, half, half, full, line), sems], flops=3 * unit)
    parts, t2 = lax.optimization_barrier((parts, t2))
    (own,) = call(total_body, of(VM, parts), of(VM, shape(parts.shape, F32)))
    every = lax.all_to_all(own, "rel", 0, 0, tiled=True)
    s2, sst2 = call(
        functools.partial(last_source_body, 1),
        of(HBM, s1, sst1, gq1, rel1, sid),
        of(HBM, full, line),
        [*room(s1, sst1, gq1, rel1, sid, full, line), sems], flops=2 * unit)
    summed = every.reshape(piece * group, rels)[:d]
    rst1 = rst + summed * summed
    r1 = r - LR * summed / (jnp.sqrt(rst1) + EPS)
    return s2, sst2, t2, tst2, r1, rst1


def solution(mesh):
    both = ("blk", "rel")
    placed = (
        P(None, both), P(both), P(None, both), P(both), P(None, "blk"), P(None, "blk"),
        P(None, both), P(None, both), P(None, both), P(None, both),
    )
    return jax.shard_map(
        per_device,
        mesh=mesh,
        in_specs=placed,
        out_specs=placed[:6],
        check_vma=False,
    )
```

```python
import functools

import jax
import jax.numpy as jnp
from jax import lax
from jax.experimental import pallas as pl
from jax.experimental.pallas import tpu as pltpu
from jax.sharding import PartitionSpec as P

LR = 0.1
EPS = 1e-06
F32 = jnp.float32
BF16 = jnp.bfloat16
VMEM_LIMIT = 32 * 1024 * 1024
TILE = 256
NEAR = 512


def split(x):
    hi = x.astype(BF16)
    lo = (x - hi.astype(F32)).astype(BF16)
    return hi, lo


def dot(a, b):
    return jnp.dot(a, b, preferred_element_type=F32)


def dot_nt(a, b):
    return lax.dot_general(a, b, (((1,), (1,)), ((), ())), preferred_element_type=F32)


def column(row):
    n = row.shape[1]
    return jnp.transpose(jnp.broadcast_to(row, (8, n)))[:, 0:1]


def hot_down(row, length):
    n = row.shape[1]
    spots = lax.broadcasted_iota(jnp.int32, (length, n), 0)
    return jnp.where(spots == row, 1.0, 0.0).astype(BF16)


def hot_along(col, length, start=0):
    n = col.shape[0]
    spots = lax.broadcasted_iota(jnp.int32, (n, length), 1) + start
    return jnp.where(spots == col, 1.0, 0.0).astype(BF16)


def picked(matrix, hot):
    hi, lo = split(matrix)
    return dot(hi, hot) + dot(lo, hot)


def scores(q_t, t):
    (qa, qb), (ta, tb) = q_t, split(t)
    return dot(qa, ta) + dot(qa, tb) + dot(qb, ta)


def weights(score, target_col, negative_col, start):
    spots = lax.broadcasted_iota(jnp.int32, score.shape, 1) + start
    share = 1.0 / negative_col.shape[0]
    count = jnp.sum(jnp.where(spots == negative_col, share, 0.0), axis=0, keepdims=True)
    level = jax.nn.sigmoid(score)
    return split(level * count + jnp.where(spots == target_col, level - 1.0, 0.0))


def stepped(matrix, state, grad):
    fresh = state + jnp.sum(grad * grad, axis=0, keepdims=True) * (1.0 / grad.shape[0])
    return matrix - grad * (LR / (jnp.sqrt(fresh) + EPS)), fresh


def started(copies):
    out = [pltpu.make_async_copy(src, dst, sem) for src, dst, sem in copies]
    for c in out:
        c.start()
    return out


def near_body(bucket, s_in, t_in, tst_in, r_in, sid_in, tid_in, rid_in, nid_in,
              near_ref, src_ref, rel_ref, qa_ref, qb_ref, qta_ref, qtb_ref, wa_ref, wb_ref,
              tfar_ref, tstfar_ref, spots_ref,
              s_ref, t_ref, tst_ref, r_ref, sid_ref, tid_ref, rid_ref, nid_ref, sems):
    d, rows = s_ref.shape
    half = d // 16 * 8
    first = started([
        (sid_in, sid_ref, sems.at[0]), (rid_in, rid_ref, sems.at[1]), (r_in, r_ref, sems.at[2]),
        (s_in.at[0:half], s_ref.at[0:half], sems.at[3]), (s_in.at[half:], s_ref.at[half:], sems.at[4])])
    for c in first[0:3]:
        c.wait()
    hot_r = hot_down(rid_ref[bucket:bucket + 1, :], r_ref.shape[1])
    hot_s = hot_down(sid_ref[bucket:bucket + 1, :], rows)
    rel = picked(r_ref[...], hot_r)
    first[3].wait()
    second = started([
        (tid_in, tid_ref, sems.at[5]), (nid_in, nid_ref, sems.at[6]), (tst_in, tst_ref, sems.at[7]),
        (t_in.at[:, 0:NEAR], t_ref, sems.at[8]), (t_in.at[:, NEAR:], tfar_ref, sems.at[9])])
    upper = picked(s_ref[0:half], hot_s)
    first[4].wait()
    src = jnp.concatenate([upper, picked(s_ref[half:], hot_s)], axis=0)
    src_ref[...] = src
    rel_ref[...] = rel
    q = src * rel
    qa, qb = split(q)
    qa_ref[...] = qa
    qb_ref[...] = qb
    q_t = split(jnp.transpose(q))
    qta_ref[...], qtb_ref[...] = q_t
    for c in second[0:4]:
        c.wait()
    target_col = column(tid_ref[bucket:bucket + 1, :])
    negative_col = column(nid_ref[bucket:bucket + 1, :])
    spots_ref[:, 0:1] = target_col
    spots_ref[:, 1:2] = negative_col
    state = tst_ref[...][None]
    tstfar_ref[...] = jnp.broadcast_to(state[:, NEAR:], tstfar_ref.shape)
    later = scores(q_t, t_ref[:, 0:TILE])
    for start in range(0, NEAR, TILE):
        cols = slice(start, start + TILE)
        score = later
        if start + TILE < NEAR:
            later = scores(q_t, t_ref[:, start + TILE:start + 2 * TILE])
        wa, wb = weights(score, target_col, negative_col, start)
        wa_ref[:, cols] = wa
        wb_ref[:, cols] = wb
        t_new, fresh = stepped(t_ref[:, cols], state[:, cols], dot(qa, wa) + dot(qb, wa) + dot(qa, wb))
        near_ref[0:d, cols] = t_new
        near_ref[d:d + 8, cols] = jnp.broadcast_to(fresh, (8, TILE))
    second[4].wait()


def far_body(t_ref, tst_ref, spots_ref, qa_ref, qb_ref, qta_ref, qtb_ref,
             far_ref, up_ref, down_ref, wa_ref, wb_ref):
    d = t_ref.shape[0]
    t, qa, qb = t_ref[...], qa_ref[...], qb_ref[...]
    score = scores((qta_ref[...], qtb_ref[...]), t)
    wa, wb = weights(score, spots_ref[:, 0:1], spots_ref[:, 1:2], NEAR)
    wa_ref[...] = wa
    wb_ref[...] = wb
    t_new, fresh = stepped(t, tst_ref[0:1, :], dot(qa, wa) + dot(qb, wa) + dot(qa, wb))
    far_ref[0:d, :] = t_new
    far_ref[d:d + 8, :] = jnp.broadcast_to(fresh, (8, t.shape[1]))
    cut = up_ref.shape[1]
    up_ref[...] = far_ref[:, 0:cut]
    down_ref[...] = far_ref[:, cut:]


def source_body(bucket, s_in, sst_in, t_in, r_in, sid_in, rid_in,
                src_ref, rel_ref, wna_ref, wnb_ref, wfa_ref, wfb_ref,
                snew_out, sst_out, rel2_out, qa_out, qb_out, rgrad_ref, src2_ref, qta_ref, qtb_ref,
                s_ref, sst_ref, t_ref, r_ref, sid_ref, rid_ref,
                snew_ref, sstnew_ref, rel2_ref, qa_ref, qb_ref, sems):
    d, rows = s_ref.shape
    copies = started([
        (t_in, t_ref, sems.at[0]), (sid_in, sid_ref, sems.at[1]), (rid_in, rid_ref, sems.at[2]),
        (r_in, r_ref, sems.at[3]), (s_in, s_ref, sems.at[4]), (sst_in, sst_ref, sems.at[5])])
    copies[0].wait()
    ta, tb = split(t_ref[:, 0:NEAR])
    gq = dot_nt(ta, wna_ref[...]) + dot_nt(tb, wna_ref[...]) + dot_nt(ta, wnb_ref[...])
    ta, tb = split(t_ref[:, NEAR:])
    gq += dot_nt(ta, wfa_ref[...]) + dot_nt(tb, wfa_ref[...]) + dot_nt(ta, wfb_ref[...])
    for c in copies[1:]:
        c.wait()
    rid_col = column(rid_ref[bucket:bucket + 1, :])
    sid_col = column(sid_ref[bucket:bucket + 1, :])
    rgrad_ref[...] = picked(gq * src_ref[...], hot_along(rid_col, r_ref.shape[1]))
    grad = picked(gq * rel_ref[...], hot_along(sid_col, rows))
    s_new, fresh = stepped(s_ref[...], sst_ref[...][None], grad)
    snew_ref[...] = s_new
    sstnew_ref[...] = fresh[0]
    outs = started([(snew_ref, snew_out, sems.at[6]), (sstnew_ref, sst_out, sems.at[7])])
    after = bucket + 1
    src = picked(s_new, hot_down(sid_ref[after:after + 1, :], rows))
    rel = picked(r_ref[...], hot_down(rid_ref[after:after + 1, :], r_ref.shape[1]))
    src2_ref[...] = src
    rel2_ref[...] = rel
    q = src * rel
    qa_ref[...], qb_ref[...] = split(q)
    outs += started([(rel2_ref, rel2_out, sems.at[8]), (qa_ref, qa_out, sems.at[9]), (qb_ref, qb_out, sems.at[10])])
    qta_ref[...], qtb_ref[...] = split(jnp.transpose(q))
    for c in outs:
        c.wait()


def query_body(bucket, direct_ref, up_ref, down_ref, near_ref, src_ref, qta_ref, qtb_ref, rgrad_ref,
               tid_ref, rid_ref, nid_ref,
               gq_ref, wa_ref, wb_ref, t_out, sum_out, far_ref, sum_ref, sems):
    d = src_ref.shape[0]
    rows = wa_ref.shape[1]
    cut = up_ref.shape[1]
    far_ref[:, 0:cut] = direct_ref[:, 0:cut] + up_ref[...]
    far_ref[:, cut:] = direct_ref[:, cut:] + down_ref[...]
    outs = started([(near_ref, t_out.at[:, 0:NEAR], sems.at[0]), (far_ref, t_out.at[:, NEAR:], sems.at[1])])
    q_t = (qta_ref[...], qtb_ref[...])
    target_col = column(tid_ref[bucket:bucket + 1, :])
    negative_col = column(nid_ref[bucket:bucket + 1, :])

    def block(start):
        if start < NEAR:
            return near_ref[0:d, start:start + TILE]
        return far_ref[0:d, start - NEAR:start - NEAR + TILE]

    gq = jnp.zeros(src_ref.shape, F32)
    later = scores(q_t, block(0))
    for start in range(0, rows, TILE):
        cols = slice(start, start + TILE)
        score = later
        if start + TILE < rows:
            later = scores(q_t, block(start + TILE))
        wa, wb = weights(score, target_col, negative_col, start)
        wa_ref[:, cols] = wa
        wb_ref[:, cols] = wb
        ta, tb = split(block(start))
        gq += dot_nt(ta, wa) + dot_nt(tb, wa) + dot_nt(ta, wb)
    gq_ref[...] = gq
    rid_col = column(rid_ref[bucket:bucket + 1, :])
    sum_ref[...] = rgrad_ref[...] + picked(gq * src_ref[...], hot_along(rid_col, rgrad_ref.shape[1]))
    outs += started([(sum_ref, sum_out.at[i], sems.at[2 + i]) for i in range(sum_out.shape[0])])
    for c in outs:
        c.wait()


def target_body(t_in, qa_in, qb_in, wa_ref, wb_ref, tnew_out, tst_out,
                t_ref, qa_ref, qb_ref, tnew_ref, tst_ref, sems):
    d, rows = tnew_ref.shape
    c_a, c_b, c_t = started([(qa_in, qa_ref, sems.at[4]), (qb_in, qb_ref, sems.at[5]), (t_in, t_ref, sems.at[6])])
    c_a.wait()
    c_b.wait()
    qa, qb = qa_ref[...], qb_ref[...]
    outs = []
    for i, start in enumerate(range(0, rows, TILE)):
        cols = slice(start, start + TILE)
        wa, wb = wa_ref[:, cols], wb_ref[:, cols]
        grad = dot(qa, wa) + dot(qb, wa) + dot(qa, wb)
        if i == 0:
            c_t.wait()
        t_new, fresh = stepped(t_ref[0:d, cols], t_ref[d:d + 1, cols], grad)
        tnew_ref[:, cols] = t_new
        tst_ref[cols] = fresh[0]
        outs += started([(tnew_ref.at[:, cols], tnew_out.at[:, cols], sems.at[1 + i])])
    outs += started([(tst_ref, tst_out, sems.at[0])])
    for c in outs:
        c.wait()


def last_source_body(bucket, s_in, sst_in, gq_ref, rel_in, sid_in, snew_out, sst_out,
                     s_ref, sst_ref, rel_ref, sid_ref, snew_ref, sstnew_ref, sems):
    d, rows = s_ref.shape
    c_sid, c_rel, c_s, c_sst = started([
        (sid_in, sid_ref, sems.at[4]), (rel_in, rel_ref, sems.at[5]), (s_in, s_ref, sems.at[6]),
        (sst_in, sst_ref, sems.at[7])])
    c_sid.wait()
    c_rel.wait()
    sid_col = column(sid_ref[bucket:bucket + 1, :])
    ga, gb = split(gq_ref[...] * rel_ref[...])
    c_s.wait()
    c_sst.wait()
    outs = []
    for i, start in enumerate(range(0, rows, TILE)):
        cols = slice(start, start + TILE)
        hot = hot_along(sid_col, TILE, start)
        s_new, fresh = stepped(s_ref[:, cols], sst_ref[cols][None], dot(ga, hot) + dot(gb, hot))
        snew_ref[:, cols] = s_new
        sstnew_ref[cols] = fresh[0]
        outs += started([(snew_ref.at[:, cols], snew_out.at[:, cols], sems.at[1 + i])])
    outs += started([(sstnew_ref, sst_out, sems.at[0])])
    for c in outs:
        c.wait()


HBM, VM = pltpu.HBM, pltpu.VMEM


def call(body, ins, outs, scratch=(), flops=0):
    moved = sum(a.size * a.dtype.itemsize for _, a in (*ins, *outs))
    return pl.pallas_call(
        body,
        out_shape=[m(a.shape, a.dtype) for m, a in outs],
        in_specs=[pl.BlockSpec(memory_space=m) for m, _ in ins],
        out_specs=[pl.BlockSpec(memory_space=m) for m, _ in outs],
        scratch_shapes=list(scratch),
        compiler_params=pltpu.CompilerParams(vmem_limit_bytes=VMEM_LIMIT),
        cost_estimate=pl.CostEstimate(flops=flops, bytes_accessed=moved, transcendentals=0),
    )(*[pltpu.with_memory_space_constraint(a, m) for m, a in ins])


def of(spec, *arrays):
    return [(spec, a) for a in arrays]


def room(*arrays):
    return [pltpu.VMEM(a.shape, a.dtype) for a in arrays]


def per_device(s, sst, t, tst, r, rst, sid, tid, rid, nid):
    d, rows = s.shape
    edges = sid.shape[1]
    rels = r.shape[1]
    away = rows - NEAR
    shape = jax.ShapeDtypeStruct
    sems = pltpu.SemaphoreType.DMA((12,))
    wide = shape((d, edges), F32)
    thin = shape((d, edges), BF16)
    thin_t = shape((edges, d), BF16)
    full = shape((d, rows), F32)
    held = shape((d + 8, rows), F32)
    line = shape((rows,), F32)
    half = shape((edges, rows), BF16)
    near_w = shape((edges, NEAR), BF16)
    far_w = shape((edges, away), BF16)
    unit = 2 * d * rows * edges

    near, src0, rel0, qa0, qb0, qta0, qtb0, wna, wnb, tfar, tstfar, spots = call(
        functools.partial(near_body, 0),
        of(HBM, s, t, tst, r, sid, tid, rid, nid),
        of(VM, shape((d + 8, NEAR), F32), wide, wide, thin, thin, thin_t, thin_t,
           near_w, near_w, shape((d, away), F32), shape((8, away), F32), shape((edges, 2), jnp.int32)),
        [*room(s, shape((d, NEAR), F32), tst, r, sid, tid, rid, nid), sems], flops=7 * unit)
    cut = away // 2
    far, up, down, wfa, wfb = call(
        far_body,
        of(VM, tfar, tstfar, spots, qa0, qb0, qta0, qtb0),
        of(VM, shape((d + 8, away), F32), shape((d + 8, cut), F32), shape((d + 8, away - cut), F32), far_w, far_w),
        flops=2 * unit)

    count = lax.axis_size("blk")
    run = 16
    ring = [(i, (i + 1) % count) for i in range(count)]
    turns = [p for p in ring if p[1] % run == 0]
    near = lax.ppermute(near, "blk", ring)
    up = lax.ppermute(up, "blk", [(a, (b + run - 2) % count) for a, b in turns])
    down = lax.ppermute(down, "blk", [(a, (b + run - 4) % count) for a, b in turns])
    direct = lax.ppermute(far, "blk", [p for p in ring if p not in turns])
    s1, sst1, rel1, qa1, qb1, rgrad0, src1, qta1, qtb1 = call(
        functools.partial(source_body, 0),
        of(HBM, s, sst, t, r, sid, rid) + of(VM, src0, rel0, wna, wnb, wfa, wfb),
        of(HBM, full, line, wide, thin, thin) + of(VM, shape((d, rels), F32), wide, thin_t, thin_t),
        [*room(s, sst, t, r, sid, rid, full, line, wide, thin, thin), sems], flops=9 * unit)
    up, down, s1 = lax.optimization_barrier((up, down, s1))
    up = lax.ppermute(up, "blk", [((b + run - 2) % count, b) for a, b in turns])
    down = lax.ppermute(down, "blk", [((b + run - 4) % count, b) for a, b in turns])

    group = lax.axis_size("rel")
    gq1, wa1, wb1, t1, total = call(
        functools.partial(query_body, 1),
        of(VM, direct, up, down, near, src1, qta1, qtb1, rgrad0, tid, rid, nid),
        of(VM, wide, half, half) + of(HBM, held, shape((group, d, rels), F32)),
        [pltpu.VMEM((d + 8, away), F32), pltpu.VMEM((d, rels), F32), sems], flops=7 * unit)
    every = lax.all_to_all(total, "rel", 0, 0, tiled=True)
    t2, tst2 = call(
        target_body,
        of(HBM, t1, qa1, qb1) + of(VM, wa1, wb1),
        of(HBM, full, line),
        [*room(held, thin, thin, full, line), sems], flops=3 * unit)
    s2, sst2 = call(
        functools.partial(last_source_body, 1),
        of(HBM, s1, sst1) + of(VM, gq1) + of(HBM, rel1, sid),
        of(HBM, full, line),
        [*room(s1, sst1, rel1, sid, full, line), sems], flops=2 * unit)
    summed = every.sum(axis=0)
    rst1 = rst + summed * summed
    r1 = r - LR * summed / (jnp.sqrt(rst1) + EPS)
    return s2, sst2, t2, tst2, r1, rst1


def solution(mesh):
    both = ("blk", "rel")
    placed = (
        P(None, both), P(both), P(None, both), P(both), P(None, "blk"), P(None, "blk"),
        P(None, both), P(None, both), P(None, both), P(None, both),
    )
    return jax.shard_map(
        per_device,
        mesh=mesh,
        in_specs=placed,
        out_specs=placed[:6],
        check_vma=False,
    )
```

```python
import functools

import jax
import jax.numpy as jnp
from jax import lax
from jax.experimental import pallas as pl
from jax.experimental.pallas import tpu as pltpu
from jax.sharding import PartitionSpec as P

LR = 0.1
EPS = 1e-06
F32 = jnp.float32
BF16 = jnp.bfloat16
VMEM_LIMIT = 32 * 1024 * 1024
TILE = 256
NEAR = 512


def split(x):
    hi = x.astype(BF16)
    lo = (x - hi.astype(F32)).astype(BF16)
    return hi, lo


def dot(a, b):
    return jnp.dot(a, b, preferred_element_type=F32)


def dot_nt(a, b):
    return lax.dot_general(a, b, (((1,), (1,)), ((), ())), preferred_element_type=F32)


def column(row):
    n = row.shape[1]
    return jnp.transpose(jnp.broadcast_to(row, (8, n)))[:, 0:1]


def hot_down(row, length):
    n = row.shape[1]
    spots = lax.broadcasted_iota(jnp.int32, (length, n), 0)
    return jnp.where(spots == row, 1.0, 0.0).astype(BF16)


def hot_along(col, length, start=0):
    n = col.shape[0]
    spots = lax.broadcasted_iota(jnp.int32, (n, length), 1) + start
    return jnp.where(spots == col, 1.0, 0.0).astype(BF16)


def picked(matrix, hot):
    hi, lo = split(matrix)
    return dot(hi, hot) + dot(lo, hot)


def scores(q_t, t):
    (qa, qb), (ta, tb) = q_t, split(t)
    return dot(qa, ta) + dot(qa, tb) + dot(qb, ta)


def weights(score, target_col, negative_col, start):
    spots = lax.broadcasted_iota(jnp.int32, score.shape, 1) + start
    share = 1.0 / negative_col.shape[0]
    count = jnp.sum(jnp.where(spots == negative_col, share, 0.0), axis=0, keepdims=True)
    level = jax.nn.sigmoid(score)
    return split(level * count + jnp.where(spots == target_col, level - 1.0, 0.0))


def stepped(matrix, state, grad):
    fresh = state + jnp.sum(grad * grad, axis=0, keepdims=True) * (1.0 / grad.shape[0])
    return matrix - grad * (LR / (jnp.sqrt(fresh) + EPS)), fresh


def started(copies):
    out = [pltpu.make_async_copy(src, dst, sem) for src, dst, sem in copies]
    for c in out:
        c.start()
    return out


def near_body(bucket, s_in, t_in, tst_in, r_in, sid_in, tid_in, rid_in, nid_in,
              near_ref, src_ref, rel_ref, qa_ref, qb_ref, qta_ref, qtb_ref, wa_ref, wb_ref,
              tfar_ref, tstfar_ref, spots_ref,
              s_ref, t_ref, tst_ref, r_ref, sid_ref, tid_ref, rid_ref, nid_ref, sems):
    d, rows = s_ref.shape
    first = started([
        (sid_in, sid_ref, sems.at[0]), (rid_in, rid_ref, sems.at[1]), (r_in, r_ref, sems.at[2]),
        (s_in, s_ref, sems.at[3])])
    for c in first[0:3]:
        c.wait()
    hot_r = hot_down(rid_ref[bucket:bucket + 1, :], r_ref.shape[1])
    hot_s = hot_down(sid_ref[bucket:bucket + 1, :], rows)
    rel = picked(r_ref[...], hot_r)
    first[3].wait()
    second = started([
        (tid_in, tid_ref, sems.at[5]), (nid_in, nid_ref, sems.at[6]), (tst_in, tst_ref, sems.at[7]),
        (t_in.at[:, 0:NEAR], t_ref, sems.at[8]), (t_in.at[:, NEAR:], tfar_ref, sems.at[9])])
    src = picked(s_ref[...], hot_s)
    src_ref[...] = src
    rel_ref[...] = rel
    q = src * rel
    qa, qb = split(q)
    qa_ref[...] = qa
    qb_ref[...] = qb
    q_t = split(jnp.transpose(q))
    qta_ref[...], qtb_ref[...] = q_t
    for c in second[0:4]:
        c.wait()
    target_col = column(tid_ref[bucket:bucket + 1, :])
    negative_col = column(nid_ref[bucket:bucket + 1, :])
    spots_ref[:, 0:1] = target_col
    spots_ref[:, 1:2] = negative_col
    state = tst_ref[...][None]
    tstfar_ref[...] = jnp.broadcast_to(state[:, NEAR:], tstfar_ref.shape)
    later = scores(q_t, t_ref[:, 0:TILE])
    for start in range(0, NEAR, TILE):
        cols = slice(start, start + TILE)
        score = later
        if start + TILE < NEAR:
            later = scores(q_t, t_ref[:, start + TILE:start + 2 * TILE])
        wa, wb = weights(score, target_col, negative_col, start)
        wa_ref[:, cols] = wa
        wb_ref[:, cols] = wb
        t_new, fresh = stepped(t_ref[:, cols], state[:, cols], dot(qa, wa) + dot(qb, wa) + dot(qa, wb))
        near_ref[0:d, cols] = t_new
        near_ref[d:d + 8, cols] = jnp.broadcast_to(fresh, (8, TILE))
    second[4].wait()


def far_body(t_ref, tst_ref, spots_ref, qa_ref, qb_ref, qta_ref, qtb_ref,
             far_ref, up_ref, down_ref, wa_ref, wb_ref):
    d = t_ref.shape[0]
    t, qa, qb = t_ref[...], qa_ref[...], qb_ref[...]
    score = scores((qta_ref[...], qtb_ref[...]), t)
    wa, wb = weights(score, spots_ref[:, 0:1], spots_ref[:, 1:2], NEAR)
    wa_ref[...] = wa
    wb_ref[...] = wb
    t_new, fresh = stepped(t, tst_ref[0:1, :], dot(qa, wa) + dot(qb, wa) + dot(qa, wb))
    far_ref[0:d, :] = t_new
    far_ref[d:d + 8, :] = jnp.broadcast_to(fresh, (8, t.shape[1]))
    cut = up_ref.shape[1]
    up_ref[...] = far_ref[:, 0:cut]
    down_ref[...] = far_ref[:, cut:]


def source_body(bucket, s_in, sst_in, t_in, r_in, sid_in, rid_in,
                src_ref, rel_ref, wna_ref, wnb_ref, wfa_ref, wfb_ref,
                snew_out, sst_out, rel2_out, qa_out, qb_out, rgrad_ref, src2_ref, qta_ref, qtb_ref,
                s_ref, sst_ref, t_ref, r_ref, sid_ref, rid_ref,
                snew_ref, sstnew_ref, rel2_ref, qa_ref, qb_ref, sems):
    d, rows = s_ref.shape
    copies = started([
        (t_in, t_ref, sems.at[0]), (sid_in, sid_ref, sems.at[1]), (rid_in, rid_ref, sems.at[2]),
        (r_in, r_ref, sems.at[3]), (s_in, s_ref, sems.at[4]), (sst_in, sst_ref, sems.at[5])])
    copies[0].wait()
    ta, tb = split(t_ref[:, 0:NEAR])
    gq = dot_nt(ta, wna_ref[...]) + dot_nt(tb, wna_ref[...]) + dot_nt(ta, wnb_ref[...])
    ta, tb = split(t_ref[:, NEAR:])
    gq += dot_nt(ta, wfa_ref[...]) + dot_nt(tb, wfa_ref[...]) + dot_nt(ta, wfb_ref[...])
    for c in copies[1:]:
        c.wait()
    rid_col = column(rid_ref[bucket:bucket + 1, :])
    sid_col = column(sid_ref[bucket:bucket + 1, :])
    rgrad_ref[...] = picked(gq * src_ref[...], hot_along(rid_col, r_ref.shape[1]))
    grad = picked(gq * rel_ref[...], hot_along(sid_col, rows))
    s_new, fresh = stepped(s_ref[...], sst_ref[...][None], grad)
    snew_ref[...] = s_new
    sstnew_ref[...] = fresh[0]
    outs = started([(snew_ref, snew_out, sems.at[6]), (sstnew_ref, sst_out, sems.at[7])])
    after = bucket + 1
    src = picked(s_new, hot_down(sid_ref[after:after + 1, :], rows))
    rel = picked(r_ref[...], hot_down(rid_ref[after:after + 1, :], r_ref.shape[1]))
    src2_ref[...] = src
    rel2_ref[...] = rel
    q = src * rel
    qa_ref[...], qb_ref[...] = split(q)
    outs += started([(rel2_ref, rel2_out, sems.at[8]), (qa_ref, qa_out, sems.at[9]), (qb_ref, qb_out, sems.at[10])])
    qta_ref[...], qtb_ref[...] = split(jnp.transpose(q))
    for c in outs:
        c.wait()


def query_body(bucket, direct_ref, up_ref, down_ref, near_ref, src_ref, qta_ref, qtb_ref, rgrad_ref,
               tid_ref, rid_ref, nid_ref,
               gq_ref, wa_ref, wb_ref, t_out, sum_out, far_ref, sum_ref, sems):
    d = src_ref.shape[0]
    rows = wa_ref.shape[1]
    cut = up_ref.shape[1]
    far_ref[:, 0:cut] = direct_ref[:, 0:cut] + up_ref[...]
    far_ref[:, cut:] = direct_ref[:, cut:] + down_ref[...]
    outs = started([(near_ref, t_out.at[:, 0:NEAR], sems.at[0]), (far_ref, t_out.at[:, NEAR:], sems.at[1])])
    q_t = (qta_ref[...], qtb_ref[...])
    target_col = column(tid_ref[bucket:bucket + 1, :])
    negative_col = column(nid_ref[bucket:bucket + 1, :])

    def block(start):
        if start < NEAR:
            return near_ref[0:d, start:start + TILE]
        return far_ref[0:d, start - NEAR:start - NEAR + TILE]

    gq = jnp.zeros(src_ref.shape, F32)
    later = scores(q_t, block(0))
    for start in range(0, rows, TILE):
        cols = slice(start, start + TILE)
        score = later
        if start + TILE < rows:
            later = scores(q_t, block(start + TILE))
        wa, wb = weights(score, target_col, negative_col, start)
        wa_ref[:, cols] = wa
        wb_ref[:, cols] = wb
        ta, tb = split(block(start))
        gq += dot_nt(ta, wa) + dot_nt(tb, wa) + dot_nt(ta, wb)
    gq_ref[...] = gq
    rid_col = column(rid_ref[bucket:bucket + 1, :])
    sum_ref[...] = rgrad_ref[...] + picked(gq * src_ref[...], hot_along(rid_col, rgrad_ref.shape[1]))
    outs += started([(sum_ref, sum_out.at[i], sems.at[2 + i]) for i in range(sum_out.shape[0])])
    for c in outs:
        c.wait()


def target_body(t_in, qa_in, qb_in, wa_ref, wb_ref, tnew_out, tst_out,
                t_ref, qa_ref, qb_ref, tnew_ref, tst_ref, sems):
    d, rows = tnew_ref.shape
    c_a, c_b, c_t = started([(qa_in, qa_ref, sems.at[4]), (qb_in, qb_ref, sems.at[5]), (t_in, t_ref, sems.at[6])])
    c_a.wait()
    c_b.wait()
    qa, qb = qa_ref[...], qb_ref[...]
    outs = []
    for i, start in enumerate(range(0, rows, TILE)):
        cols = slice(start, start + TILE)
        wa, wb = wa_ref[:, cols], wb_ref[:, cols]
        grad = dot(qa, wa) + dot(qb, wa) + dot(qa, wb)
        if i == 0:
            c_t.wait()
        t_new, fresh = stepped(t_ref[0:d, cols], t_ref[d:d + 1, cols], grad)
        tnew_ref[:, cols] = t_new
        tst_ref[cols] = fresh[0]
        outs += started([(tnew_ref.at[:, cols], tnew_out.at[:, cols], sems.at[1 + i])])
    outs += started([(tst_ref, tst_out, sems.at[0])])
    for c in outs:
        c.wait()


def last_source_body(bucket, s_in, sst_in, gq_ref, rel_in, sid_in, snew_out, sst_out,
                     s_ref, sst_ref, rel_ref, sid_ref, snew_ref, sstnew_ref, sems):
    d, rows = s_ref.shape
    c_sid, c_rel, c_s, c_sst = started([
        (sid_in, sid_ref, sems.at[4]), (rel_in, rel_ref, sems.at[5]), (s_in, s_ref, sems.at[6]),
        (sst_in, sst_ref, sems.at[7])])
    c_sid.wait()
    c_rel.wait()
    sid_col = column(sid_ref[bucket:bucket + 1, :])
    ga, gb = split(gq_ref[...] * rel_ref[...])
    c_s.wait()
    c_sst.wait()
    outs = []
    for i, start in enumerate(range(0, rows, TILE)):
        cols = slice(start, start + TILE)
        hot = hot_along(sid_col, TILE, start)
        s_new, fresh = stepped(s_ref[:, cols], sst_ref[cols][None], dot(ga, hot) + dot(gb, hot))
        snew_ref[:, cols] = s_new
        sstnew_ref[cols] = fresh[0]
        outs += started([(snew_ref.at[:, cols], snew_out.at[:, cols], sems.at[1 + i])])
    outs += started([(sstnew_ref, sst_out, sems.at[0])])
    for c in outs:
        c.wait()


HBM, VM = pltpu.HBM, pltpu.VMEM


def call(body, ins, outs, scratch=(), flops=0):
    moved = sum(a.size * a.dtype.itemsize for _, a in (*ins, *outs))
    return pl.pallas_call(
        body,
        out_shape=[m(a.shape, a.dtype) for m, a in outs],
        in_specs=[pl.BlockSpec(memory_space=m) for m, _ in ins],
        out_specs=[pl.BlockSpec(memory_space=m) for m, _ in outs],
        scratch_shapes=list(scratch),
        compiler_params=pltpu.CompilerParams(vmem_limit_bytes=VMEM_LIMIT),
        cost_estimate=pl.CostEstimate(flops=flops, bytes_accessed=moved, transcendentals=0),
    )(*[pltpu.with_memory_space_constraint(a, m) for m, a in ins])


def of(spec, *arrays):
    return [(spec, a) for a in arrays]


def room(*arrays):
    return [pltpu.VMEM(a.shape, a.dtype) for a in arrays]


def per_device(s, sst, t, tst, r, rst, sid, tid, rid, nid):
    d, rows = s.shape
    edges = sid.shape[1]
    rels = r.shape[1]
    away = rows - NEAR
    shape = jax.ShapeDtypeStruct
    sems = pltpu.SemaphoreType.DMA((12,))
    wide = shape((d, edges), F32)
    thin = shape((d, edges), BF16)
    thin_t = shape((edges, d), BF16)
    full = shape((d, rows), F32)
    held = shape((d + 8, rows), F32)
    line = shape((rows,), F32)
    half = shape((edges, rows), BF16)
    near_w = shape((edges, NEAR), BF16)
    far_w = shape((edges, away), BF16)
    unit = 2 * d * rows * edges

    near, src0, rel0, qa0, qb0, qta0, qtb0, wna, wnb, tfar, tstfar, spots = call(
        functools.partial(near_body, 0),
        of(HBM, s, t, tst, r, sid, tid, rid, nid),
        of(VM, shape((d + 8, NEAR), F32), wide, wide, thin, thin, thin_t, thin_t,
           near_w, near_w, shape((d, away), F32), shape((8, away), F32), shape((edges, 2), jnp.int32)),
        [*room(s, shape((d, NEAR), F32), tst, r, sid, tid, rid, nid), sems], flops=7 * unit)
    cut = away // 2
    far, up, down, wfa, wfb = call(
        far_body,
        of(VM, tfar, tstfar, spots, qa0, qb0, qta0, qtb0),
        of(VM, shape((d + 8, away), F32), shape((d + 8, cut), F32), shape((d + 8, away - cut), F32), far_w, far_w),
        flops=2 * unit)

    count = lax.axis_size("blk")
    run = 16
    ring = [(i, (i + 1) % count) for i in range(count)]
    turns = [p for p in ring if p[1] % run == 0]
    near = lax.ppermute(near, "blk", ring)
    up = lax.ppermute(up, "blk", [(a, (b + run - 2) % count) for a, b in turns])
    down = lax.ppermute(down, "blk", [(a, (b + run - 4) % count) for a, b in turns])
    direct = lax.ppermute(far, "blk", [p for p in ring if p not in turns])
    s1, sst1, rel1, qa1, qb1, rgrad0, src1, qta1, qtb1 = call(
        functools.partial(source_body, 0),
        of(HBM, s, sst, t, r, sid, rid) + of(VM, src0, rel0, wna, wnb, wfa, wfb),
        of(HBM, full, line, wide, thin, thin) + of(VM, shape((d, rels), F32), wide, thin_t, thin_t),
        [*room(s, sst, t, r, sid, rid, full, line, wide, thin, thin), sems], flops=9 * unit)
    up, down, s1 = lax.optimization_barrier((up, down, s1))
    up = lax.ppermute(up, "blk", [((b + run - 2) % count, b) for a, b in turns])
    down = lax.ppermute(down, "blk", [((b + run - 4) % count, b) for a, b in turns])

    group = lax.axis_size("rel")
    gq1, wa1, wb1, t1, total = call(
        functools.partial(query_body, 1),
        of(VM, direct, up, down, near, src1, qta1, qtb1, rgrad0, tid, rid, nid),
        of(VM, wide, half, half) + of(HBM, held, shape((group, d, rels), F32)),
        [pltpu.VMEM((d + 8, away), F32), pltpu.VMEM((d, rels), F32), sems], flops=7 * unit)
    every = lax.all_to_all(total, "rel", 0, 0, tiled=True)
    t2, tst2 = call(
        target_body,
        of(HBM, t1, qa1, qb1) + of(VM, wa1, wb1),
        of(HBM, full, line),
        [*room(held, thin, thin, full, line), sems], flops=3 * unit)
    s2, sst2 = call(
        functools.partial(last_source_body, 1),
        of(HBM, s1, sst1) + of(VM, gq1) + of(HBM, rel1, sid),
        of(HBM, full, line),
        [*room(s1, sst1, rel1, sid, full, line), sems], flops=2 * unit)
    summed = every.sum(axis=0)
    rst1 = rst + summed * summed
    r1 = r - LR * summed / (jnp.sqrt(rst1) + EPS)
    return s2, sst2, t2, tst2, r1, rst1


def solution(mesh):
    both = ("blk", "rel")
    placed = (
        P(None, both), P(both), P(None, both), P(both), P(None, "blk"), P(None, "blk"),
        P(None, both), P(None, both), P(None, both), P(None, both),
    )
    return jax.shard_map(
        per_device,
        mesh=mesh,
        in_specs=placed,
        out_specs=placed[:6],
        check_vma=False,
    )
```
